32 devices in a mesh: fsdp: 4 (over y, core), expert: 8 (over z, x).
Axes of the slice: x: 2, y: 2, z: 4, core: 2. Of those that a mesh axis runs over, the one named last changes fastest.
Arguments:
- tokens: bfloat16 [512, 4096], P(('fsdp', 'expert')), may hold values from -18 to 18
- learner_rows: bfloat16 [16, 3, 768, 4096], P(None, None, 'expert', 'fsdp'), may hold values from -0.25 to 0.25, as said below
- exponents: int32 [16, 3, 768, 128], P(None, None, 'expert', 'fsdp'), may hold values from -9 to -5
- expert_ids: int32 [512, 8], P(('fsdp', 'expert')), may hold values from 0 to 15, all different within a row; in each aligned block of 16 rows (0 to 15, 16 to 31, ...) at most 16 rows name the same one
- route_probs: float32 [512, 8], P(('fsdp', 'expert')), may hold values from 0.05 to 1
Outputs:
- rollout_elements: bfloat16 [16, 3, 768, 4096], P('expert', None, None, 'fsdp')
- mixed: bfloat16 [512, 4096], P(('fsdp', 'expert'))
The draws below stay inside these ranges and needn't reach their ends.
Inputs may be any that keep to these rules, and one draw needn't show every extreme that they name: `expert_ids`: each row names 8 different experts. Among the rows of one device no expert is named more than 16 times, a bound that some block reaches. `learner_rows`: each entry is at most 8 times its block's scale 2 ** exponent in magnitude.
All inputs are finite; a program needn't handle non-finite values.
Results may differ from the reference program's by a relative error of at most 0.02.
Values may be sent and summed in bfloat16 or wider, within the bound.
No kernel may reach another device: no remote copies, remote signals or barrier semaphores. Data moves between devices by JAX's collectives and lax.ppermute only.
A program may use at most 128 MiB of HBM per device.

```python
import math
import jax
import jax.numpy as jnp
import numpy as np
from jax import lax

D = 4096
FF = 768
TOP = 8
BLOCK = 32
TOK_DEV = 16
E = 16
CAP = 16
TOKENS = 512
N_FSDP = 4
N_EXPERT = 8


def shared_exponents(key):
    return jax.random.randint(jax.random.fold_in(key, 11), (E, 3, FF, D // BLOCK), -9, -4, dtype=jnp.int32)


def draw_exponents(key, part):
    return shared_exponents(key)


def draw_learner_rows(key, part):
    exps = shared_exponents(key)
    second = jax.random.fold_in(key, 23)
    shape = (E, 3, FF, D)
    factor = jnp.clip(1.6 * jax.random.normal(second, shape, jnp.float32), -8.0, 8.0)
    widened = jnp.repeat(jnp.exp2(exps.astype(jnp.float32)), BLOCK, axis=3)
    return (factor * widened).astype(jnp.bfloat16)


def levels(own_key, dims, cuts, least, high):
    loudness = 1.0
    for axis_at, shards_of in cuts:
        steps = jax.random.uniform(jax.random.fold_in(jax.random.fold_in(own_key, 6), axis_at), (shards_of,), jnp.float32, least / len(cuts), high / len(cuts))
        loudness = loudness * jnp.repeat(jnp.exp(steps), dims[axis_at] // shards_of).reshape((-1,) + (1,) * (len(dims) - 1 - axis_at))
    return loudness


def routed_block(key, own, number, rows, amount, top, reach, slope):
    order = jax.random.permutation(key, amount)
    heavy_load, usual = shares(amount, rows * top, reach, slope, True), shares(amount, rows * top, reach, slope, False)
    places = jnp.arange(amount)

    def named(lengths, offset_by):
        used = int((lengths > 0).sum())
        fixed = max(1, used // 4)
        passed = fixed + (places - fixed + offset_by * (used - fixed)) % max(1, amount - fixed)
        return jnp.zeros((amount,), jnp.int32).at[order[jnp.where(places < fixed, places, passed)]].set(jnp.asarray(lengths, jnp.int32))

    lengths = jnp.where(number % 4 == 0, named(heavy_load, number // 4), named(usual, number - number // 4 - 1))
    mixed = jax.random.permutation(jax.random.fold_in(own, 3), amount)
    giver, receiver = mixed[0:amount // 2 * 2:2], mixed[1:amount // 2 * 2:2]
    slack = jnp.minimum(lengths[giver] - 1, reach - lengths[receiver]) // 2
    slack = jnp.where((giver == order[0]) | (receiver == order[0]) | (lengths[receiver] == 0), 0, jnp.maximum(slack, 0))
    passed = jax.random.randint(jax.random.fold_in(own, 4), (amount // 2,), 0, 1 << 20) % (slack + 1)
    lengths = lengths.at[giver].add(-passed).at[receiver].add(passed)
    members = jnp.searchsorted(jnp.cumsum(lengths), jnp.arange(rows * top), side="right").astype(jnp.int32)
    grid = members.reshape(top, rows).T
    grid = grid[jax.random.permutation(jax.random.fold_in(own, 1), rows)]
    offset_by = jax.random.randint(jax.random.fold_in(own, 2), (rows, 1), 0, top)
    return jnp.take_along_axis(grid, (jnp.arange(top)[None, :] + offset_by) % top, axis=1)


def shares(number_of, total, most, slope, full):
    portions = [(1 << 20) // math.isqrt(standing ** slope) + 1 for standing in range(1, number_of + 1)]
    largest = most if full else min(most, max(-(-total // number_of), total * portions[0] // sum(portions)))
    least = 1 if total - largest >= number_of - 1 else 0
    holding, surplus = [largest] + [least] * (number_of - 1), total - largest - least * (number_of - 1)
    while surplus > 0:
        movable = [i for i in range(1, number_of) if holding[i] < largest] or [i for i in range(1, number_of) if holding[i] < most]
        pool, left = sum([portions[i] for i in movable]), surplus
        for i in movable:
            addition = min(most - holding[i], max(1, left * portions[i] // pool), surplus)
            holding[i] = holding[i] + addition
            surplus = surplus - addition
    return np.array(holding)


def scatter_about(rng, dims, deviation, most, cuts=(), kind=jnp.bfloat16):
    level = levels(rng, dims, cuts, -0.22, 0.18) if cuts else 1.0
    values = jax.random.normal(rng, dims, jnp.float32) * deviation * level
    return jnp.minimum(jnp.maximum(values, -most), most).astype(kind)


def setup_inputs(seed: int = 0) -> dict:
    key_of = jax.random.split(jax.random.key(seed), 6)
    tokens = scatter_about(key_of[0], (TOKENS, D), 3.0, 18.0, ((0, 32),))
    learner_rows = draw_learner_rows(jax.random.fold_in(key_of[5], 71), 0)
    exponents = draw_exponents(jax.random.fold_in(key_of[5], 71), 0)
    expert_ids_keys = jax.random.split(jax.random.fold_in(key_of[3], 1), TOKENS // TOK_DEV)
    expert_ids_turns = jax.random.permutation(jax.random.fold_in(key_of[3], 3), TOKENS // TOK_DEV)
    expert_ids = jax.vmap(lambda own, number: routed_block(jax.random.fold_in(key_of[3], 2), own, number, TOK_DEV, E, TOP, CAP, 2))(expert_ids_keys, expert_ids_turns).reshape((TOKENS, TOP))
    route_probs = jnp.clip(jnp.exp(math.log(1.0) - 2.9957323 * jax.random.uniform(key_of[4], (TOKENS, TOP), jnp.float32) ** levels(key_of[4], (TOKENS, TOP), ((0, 32),), -0.2, 0.2)), 0.05, 1.0)
    return dict(tokens=tokens, learner_rows=learner_rows, exponents=exponents, expert_ids=expert_ids, route_probs=route_probs)


def to_grid(ratio):
    clipped = jnp.clip(ratio.astype(jnp.float32), -6.0, 6.0)
    magnitude = jnp.abs(clipped)
    level = 0.5 * (magnitude > 0.25) + 0.5 * (magnitude >= 0.75) + 0.5 * (magnitude > 1.25) + 0.5 * (magnitude >= 1.75)
    level = level + 1.0 * (magnitude > 2.5) + 1.0 * (magnitude >= 3.5) + 2.0 * (magnitude > 5.0)
    return (jnp.sign(clipped) * level.astype(jnp.float32)).astype(jnp.bfloat16)


def encode(pieces):
    rows_part, exponent = pieces
    widened = jnp.repeat(jnp.exp2(exponent.astype(jnp.float32)).astype(jnp.bfloat16), BLOCK, axis=2)
    return to_grid(rows_part / widened)


def reference(tokens, learner_rows, exponents, expert_ids, route_probs):
    devices = N_FSDP * N_EXPERT
    capacity = 2 * TOK_DEV * TOP // E
    rollout_elements = lax.map(encode, (learner_rows, exponents))
    routes = expert_ids.reshape(devices, TOK_DEV * TOP)
    one_hot = (routes[:, :, None] == jnp.arange(E, dtype=jnp.int32)[None, None, :]).astype(jnp.int32)
    position = jnp.sum((jnp.cumsum(one_hot, axis=1) - one_hot) * one_hot, axis=2)
    slot_index = (jnp.arange(devices, dtype=jnp.int32)[:, None] * capacity + position).astype(jnp.int32)
    token_index = jnp.repeat(jnp.arange(TOKENS, dtype=jnp.int32), TOP)
    route_share = route_probs / jnp.sum(route_probs, axis=1, keepdims=True)
    flat_routes = routes.reshape(-1)
    flat_slots = slot_index.reshape(-1)
    table = jnp.full((E, devices * capacity), TOKENS, dtype=jnp.int32).at[flat_routes, flat_slots].set(token_index)
    weight = jnp.zeros((E, devices * capacity), jnp.float32).at[flat_routes, flat_slots].set(route_share.reshape(-1))
    padded = jnp.concatenate([tokens, jnp.zeros((1, D), jnp.bfloat16)], axis=0)
    slot_total = devices * capacity

    def apply_expert(running, pieces):
        elements, exponent, rows_index, rows_weight = pieces
        widened = jnp.repeat(jnp.exp2(exponent.astype(jnp.float32)).astype(jnp.bfloat16), BLOCK, axis=2)
        weights = elements * widened
        gathered = padded[rows_index]
        blocks = gathered.astype(jnp.float32).reshape(slot_total, N_FSDP, D // N_FSDP)
        paired = weights[0:2].astype(jnp.float32).reshape(2, FF, N_FSDP, D // N_FSDP)
        partial_value = jnp.einsum("rfd,ghfd->gfrh", blocks, paired, precision=lax.Precision.HIGHEST)
        partial_value = lax.optimization_barrier(partial_value.astype(jnp.bfloat16)).astype(jnp.float32)
        summed = jnp.sum(partial_value, axis=1)
        hidden = (jax.nn.silu(summed[0]) * summed[1]).astype(jnp.bfloat16)
        output = jnp.dot(hidden, weights[2], preferred_element_type=jnp.float32).astype(jnp.bfloat16)
        running = running.at[rows_index].add(rows_weight[:, None] * output.astype(jnp.float32), mode="drop")
        return running, None

    mixed, _ = lax.scan(apply_expert, jnp.zeros((TOKENS, D), jnp.float32), (rollout_elements, exponents, table, weight))
    return rollout_elements, mixed.astype(jnp.bfloat16)
```

```python
import functools

import jax
import jax.numpy as jnp
from jax import lax
from jax.experimental import pallas as pl
from jax.experimental.pallas import tpu as pltpu
from jax.sharding import PartitionSpec as P

HALVES, ONES, TWOS = 1.5 * 2.0**22, 1.5 * 2.0**23, 1.5 * 2.0**24


def spread(values, width):
    blocks = values.shape[1]
    shape = (blocks, width)
    feature = lax.broadcasted_iota(jnp.int32, shape, 1)
    block = lax.broadcasted_iota(jnp.int32, shape, 0)
    size = width // blocks
    inside = (feature >= block * size) & (feature < (block + 1) * size)
    table = inside.astype(jnp.float32).astype(jnp.bfloat16)
    return jnp.dot(values.astype(jnp.bfloat16), table, preferred_element_type=jnp.float32)


def to_grid(rows, exponent):
    one = jnp.ones_like(exponent)
    inverse = lax.shift_left(one, -exponent).astype(jnp.float32)
    ratio = rows.astype(jnp.float32) * spread(inverse, rows.shape[1])
    ratio = jnp.clip(ratio, -6.0, 6.0)
    magnitude = jnp.abs(ratio)
    magic = jnp.where(magnitude < 2.0, HALVES, jnp.where(magnitude < 4.0, ONES, TWOS))
    return (ratio + magic) - magic


def encode_kernel(places, rows_ref, exponent_ref, out_ref):
    for part in range(rows_ref.shape[1]):
        value = to_grid(rows_ref[0, part], exponent_ref[0, part])
        out_ref[0, part] = value.astype(out_ref.dtype)


def encode(learner_rows, exponents, dest, row_block, out_rows):
    experts, parts, unit_rows, width = learner_rows.shape
    blocks = exponents.shape[3]
    per_owner = experts // lax.axis_size("expert")
    places = jnp.stack([dest, row_block]).astype(jnp.int32)
    return pl.pallas_call(
        encode_kernel,
        out_shape=jax.ShapeDtypeStruct((per_owner, parts, out_rows, width), learner_rows.dtype),
        grid_spec=pltpu.PrefetchScalarGridSpec(
            num_scalar_prefetch=1,
            grid=(per_owner,),
            in_specs=[
                pl.BlockSpec(
                    (1, parts, unit_rows, width), lambda i, s: (s[0] * per_owner + i, 0, 0, 0)
                ),
                pl.BlockSpec(
                    (1, parts, unit_rows, blocks), lambda i, s: (s[0] * per_owner + i, 0, 0, 0)
                ),
            ],
            out_specs=pl.BlockSpec((1, parts, unit_rows, width), lambda i, s: (i, 0, s[1], 0)),
        ),
        cost_estimate=pl.CostEstimate(
            flops=40 * per_owner * parts * unit_rows * width,
            bytes_accessed=4 * per_owner * parts * unit_rows * width,
            transcendentals=0,
        ),
    )(places, learner_rows, exponents)


def weights_kernel(rows_ref, exponent_ref, gate_ref, up_ref, down_ref):
    for part, ref in enumerate((gate_ref, up_ref, down_ref)):
        exponent = exponent_ref[0, part]
        value = to_grid(rows_ref[0, part], exponent)
        scale = jnp.exp2(exponent.astype(jnp.float32))
        ref[0] = (value * spread(scale, value.shape[1])).astype(ref.dtype)


def dequantize(learner_rows, exponents):
    experts, parts, unit_rows, width = learner_rows.shape
    blocks = exponents.shape[3]
    shape = jax.ShapeDtypeStruct((experts, unit_rows, width), learner_rows.dtype)
    spec = pl.BlockSpec((1, unit_rows, width), lambda i: (i, 0, 0))
    return pl.pallas_call(
        weights_kernel,
        out_shape=(shape,) * parts,
        grid=(experts,),
        in_specs=[
            pl.BlockSpec((1, parts, unit_rows, width), lambda i: (i, 0, 0, 0)),
            pl.BlockSpec((1, parts, unit_rows, blocks), lambda i: (i, 0, 0, 0)),
        ],
        out_specs=(spec,) * parts,
        cost_estimate=pl.CostEstimate(
            flops=50 * learner_rows.size,
            bytes_accessed=4 * learner_rows.size,
            transcendentals=0,
        ),
    )(learner_rows, exponents)


def swap(value, axis, bit):
    return lax.ppermute(value, axis, [(i, i ^ bit) for i in range(lax.axis_size(axis))])


def body(tokens, learner_rows, exponents, expert_ids, route_probs):
    experts, parts, unit_rows, width = learner_rows.shape
    owners = lax.axis_size("expert")
    groups = lax.axis_size("fsdp")
    per_owner = experts // owners
    tok_rows, model = tokens.shape
    me = lax.axis_index("expert")

    bits = [1 << b for b in reversed(range(owners.bit_length() - 1))]
    half = bits[0]

    order = [half + d for d in range(half)] + list(range(1, half))
    arrived = {}
    for d in order:
        sent = encode(learner_rows, exponents, me ^ d, jnp.int32(0), unit_rows)
        arrived[d] = swap(sent, "expert", d)
    elements = encode(learner_rows, exponents, me, me, owners * unit_rows)
    for d in order:
        elements = lax.dynamic_update_slice(
            elements, arrived[d], (0, 0, (me ^ d) * unit_rows, 0)
        )

    held = tokens[None]
    z_bits = bits[: (len(bits) + 1) // 2]
    for bit in z_bits:
        held = jnp.concatenate([held, swap(held, "expert", bit)], axis=0)
    slots = held.shape[0]
    held = held.reshape(slots * tok_rows, groups, width).transpose(1, 0, 2)
    held = lax.all_to_all(held, "fsdp", split_axis=0, concat_axis=0, tiled=True)
    for bit in bits[len(z_bits) :]:
        held = jnp.concatenate([held, swap(held, "expert", bit)], axis=1)
    rows = held.reshape(-1, width)

    gate_w, up_w, down_w = dequantize(learner_rows, exponents)
    nt = (((1,), (1,)), ((), ()))
    partial = jnp.stack(
        [
            lax.dot_general(
                rows, w.reshape(-1, width), nt, preferred_element_type=jnp.float32
            ).astype(jnp.bfloat16)
            for w in (gate_w, up_w)
        ],
        axis=1,
    )
    partial = partial.reshape(groups, -1, 2 * experts * unit_rows)
    summed = lax.psum_scatter(partial, "fsdp", scatter_dimension=0, tiled=False)
    summed = summed.astype(jnp.float32).reshape(-1, 2, experts * unit_rows)
    hidden = jax.nn.silu(summed[:, 0]) * summed[:, 1]

    share = route_probs / jnp.sum(route_probs, axis=1, keepdims=True)
    named = expert_ids[:, :, None] == jnp.arange(experts, dtype=jnp.int32)[None, None, :]
    table = jnp.sum(jnp.where(named, share[:, :, None], 0.0), axis=1)
    tables = lax.all_gather(table, "expert", axis=0, tiled=False)
    slot_of = [0]
    for bit in bits:
        slot_of = slot_of + [s | bit for s in slot_of]
    table = jnp.concatenate(
        [lax.dynamic_index_in_dim(tables, me ^ s, 0, keepdims=False) for s in slot_of], axis=0
    )
    shared = hidden.reshape(-1, experts, unit_rows) * table[:, :, None]
    shared = shared.astype(jnp.bfloat16).reshape(-1, experts * unit_rows)
    shared = lax.all_gather(shared, "fsdp", axis=0, tiled=True)
    out = jnp.dot(shared, down_w.reshape(-1, width), preferred_element_type=jnp.float32)

    out = out.reshape(groups, owners, tok_rows, width)
    for bit in reversed(bits):
        slots = out.shape[1] // 2
        out = out[:, :slots] + swap(out[:, slots:].astype(jnp.bfloat16), "expert", bit)
    mixed = lax.all_to_all(
        out[:, 0].astype(jnp.bfloat16), "fsdp", split_axis=0, concat_axis=0, tiled=True
    )
    mixed = mixed.transpose(1, 0, 2).reshape(tok_rows, model)
    return elements, mixed


def solution(mesh):
    return jax.shard_map(
        body,
        mesh=mesh,
        in_specs=(
            P(("fsdp", "expert"), None),
            P(None, None, "expert", "fsdp"),
            P(None, None, "expert", "fsdp"),
            P(("fsdp", "expert"), None),
            P(("fsdp", "expert"), None),
        ),
        out_specs=(P("expert", None, None, "fsdp"), P(("fsdp", "expert"), None)),
        check_vma=False,
    )
```

```python
import functools

import jax
import jax.numpy as jnp
from jax import lax
from jax.experimental import pallas as pl
from jax.experimental.pallas import tpu as pltpu
from jax.sharding import PartitionSpec as P

HALVES, ONES, TWOS = 1.5 * 2.0**22, 1.5 * 2.0**23, 1.5 * 2.0**24


def spread(values, width):
    blocks = values.shape[0]
    shape = (blocks, width)
    feature = lax.broadcasted_iota(jnp.int32, shape, 1)
    block = lax.broadcasted_iota(jnp.int32, shape, 0)
    size = width // blocks
    inside = (feature >= block * size) & (feature < (block + 1) * size)
    table = inside.astype(jnp.float32).astype(jnp.bfloat16)
    return lax.dot_general(
        values.astype(jnp.bfloat16),
        table,
        (((0,), (0,)), ((), ())),
        preferred_element_type=jnp.float32,
    )


def to_grid(rows, exponent):
    one = jnp.ones_like(exponent)
    inverse = lax.shift_left(one, -exponent).astype(jnp.float32)
    ratio = rows.astype(jnp.float32) * spread(inverse, rows.shape[1])
    ratio = jnp.clip(ratio, -6.0, 6.0)
    magnitude = jnp.abs(ratio)
    magic = jnp.where(magnitude < 2.0, HALVES, jnp.where(magnitude < 4.0, ONES, TWOS))
    return (ratio + magic) - magic


def encode_kernel(me, rows_ref, exponent_ref, out_ref):
    for part in range(rows_ref.shape[1]):
        value = to_grid(rows_ref[0, part], exponent_ref[0, part])
        out_ref[0, part] = value.astype(out_ref.dtype)


def encode(learner_rows, exponents, me, partner, first, count, out_rows, out_block):
    experts, parts, unit_rows, width = learner_rows.shape
    blocks = exponents.shape[2]
    per_owner = experts // lax.axis_size("expert")

    def place(i, s):
        return ((s[0] ^ partner) * per_owner + first + i, 0, 0, 0)

    return pl.pallas_call(
        encode_kernel,
        out_shape=jax.ShapeDtypeStruct((count, parts, out_rows, width), learner_rows.dtype),
        grid_spec=pltpu.PrefetchScalarGridSpec(
            num_scalar_prefetch=1,
            grid=(count,),
            in_specs=[
                pl.BlockSpec((1, parts, unit_rows, width), place),
                pl.BlockSpec((1, parts, blocks, unit_rows), place),
            ],
            out_specs=pl.BlockSpec(
                (1, parts, unit_rows, width), lambda i, s: (i, 0, out_block(s[0]), 0)
            ),
        ),
        cost_estimate=pl.CostEstimate(
            flops=20 * count * parts * unit_rows * width,
            bytes_accessed=4 * count * parts * unit_rows * width,
            transcendentals=0,
        ),
    )(me, learner_rows, exponents)


def weights_kernel(first, rows_ref, exponent_ref, out_ref):
    for part in range(out_ref.shape[0]):
        exponent = exponent_ref[0, part]
        value = to_grid(rows_ref[0, part], exponent)
        scale = jnp.exp2(exponent.astype(jnp.float32))
        out_ref[part, 0] = (value * spread(scale, value.shape[1])).astype(out_ref.dtype)


def dequantize(learner_rows, exponents, first, count):
    experts, parts, unit_rows, width = learner_rows.shape
    blocks = exponents.shape[2]
    size = count * experts * unit_rows * width
    return pl.pallas_call(
        functools.partial(weights_kernel, first),
        out_shape=jax.ShapeDtypeStruct((count, experts, unit_rows, width), learner_rows.dtype),
        grid=(experts,),
        in_specs=[
            pl.BlockSpec((1, count, unit_rows, width), lambda i: (i, first // count, 0, 0)),
            pl.BlockSpec((1, count, blocks, unit_rows), lambda i: (i, first // count, 0, 0)),
        ],
        out_specs=pl.BlockSpec((count, 1, unit_rows, width), lambda i: (0, i, 0, 0)),
        cost_estimate=pl.CostEstimate(
            flops=25 * size, bytes_accessed=4 * size, transcendentals=0
        ),
    )(learner_rows, exponents)


def place(elements, block, me, partner):
    row = (me[0] ^ partner) * block.shape[2]
    return lax.dynamic_update_slice(elements, block, (0, 0, row, 0))


def swap(value, axis, bit):
    return lax.ppermute(value, axis, [(i, i ^ bit) for i in range(lax.axis_size(axis))])


def together(*values):
    return lax.optimization_barrier(values)


def masks(axis):
    return [1 << b for b in reversed(range(lax.axis_size(axis).bit_length() - 1))]


def low_bits(axis):
    bits = masks(axis)
    return bits[len(bits) - len(bits) // 2 :]


def share_table(expert_ids, route_probs, experts):
    share = route_probs / jnp.sum(route_probs, axis=1, keepdims=True)
    named = expert_ids[:, :, None] == jnp.arange(experts, dtype=jnp.int32)[None, None, :]
    table = jnp.sum(jnp.where(named, share[:, :, None], 0.0), axis=1)
    pieces = []
    for _ in range(3):
        piece = lax.reduce_precision(table, 8, 7)
        table = table - piece
        pieces.append(piece.astype(jnp.bfloat16))
    pieces = jnp.concatenate(pieces, axis=1)
    return jnp.pad(pieces, ((0, 0), (0, -pieces.shape[1] % 128)))


def gather(value, axis, bits):
    for bit in bits:
        value = jnp.concatenate([value, swap(value, axis, bit)], axis=0)
    return value


def halve(value, axis, bits):
    for bit in reversed(bits):
        kept = value.shape[0] // 2
        got = swap(value[kept:].astype(jnp.bfloat16), axis, bit)
        value = value[:kept].astype(jnp.float32) + got.astype(jnp.float32)
    return value


def columns(value, bits):
    group = lax.axis_index("fsdp")
    for bit in bits:
        kept = value.shape[1] // 2
        low, high = value[:, :kept], value[:, kept:]
        upper = (group & bit) != 0
        mine, other = jnp.where(upper, high, low), jnp.where(upper, low, high)
        value = jnp.concatenate([mine, swap(other, "fsdp", bit)], axis=0)
    return value


def uncolumns(value, bits):
    group = lax.axis_index("fsdp")
    for bit in reversed(bits):
        kept = value.shape[0] // 2
        mine, other = value[:kept], swap(value[kept:], "fsdp", bit)
        upper = (group & bit) != 0
        value = jnp.concatenate(
            [jnp.where(upper, other, mine), jnp.where(upper, mine, other)], axis=1
        )
    return value


def layer(held, learner_rows, exponents, encode_more):
    experts, parts, unit_rows, width = learner_rows.shape
    groups = lax.axis_size("fsdp")
    x_bits, group_bits = low_bits("expert"), masks("fsdp")
    units = experts * unit_rows
    rows = held.shape[0]
    slots = rows << len(x_bits)

    table = held[:, groups * width :]
    held = columns(held[:, : groups * width], group_bits).reshape(groups, rows, width)
    pair = dequantize(learner_rows, exponents, 0, 2)
    for bit in x_bits:
        held = jnp.concatenate([held, swap(held, "expert", bit)], axis=1)
    held, pair, table = together(held, pair, table)
    table = gather(table, "expert", x_bits)
    partial = lax.dot_general(
        held.reshape(groups * slots, width),
        pair.reshape(-1, width),
        (((1,), (1,)), ((), ())),
        preferred_element_type=jnp.float32,
    ).astype(jnp.bfloat16)
    partial, table = together(partial, table)
    table = table[:, : 3 * experts].astype(jnp.float32).reshape(-1, 3, experts).sum(axis=1)

    down = dequantize(learner_rows, exponents, 2, 1)
    partial = halve(partial, "fsdp", group_bits)
    partial, down = together(partial, down)
    hidden = jax.nn.silu(partial[:, :units]) * partial[:, units:]
    shared = hidden.reshape(-1, experts, unit_rows) * table[:, :, None]
    shared = shared.astype(jnp.bfloat16).reshape(-1, units)
    middle = len(encode_more) // 2
    more = [make() for make in encode_more]
    shared, *first = together(gather(shared, "fsdp", group_bits), *more[:middle])
    out = jnp.dot(shared, down.reshape(-1, width), preferred_element_type=jnp.float32)
    out = out.reshape(groups, slots, width)
    for bit in reversed(x_bits):
        kept = out.shape[1] // 2
        out = out[:, :kept] + swap(out[:, kept:].astype(jnp.bfloat16), "expert", bit)
    out, *second = together(out, *more[middle:])
    return out, *first, *second


def body(tokens, learner_rows, exponents, expert_ids, route_probs):
    experts, parts, unit_rows, width = learner_rows.shape
    owners = lax.axis_size("expert")
    groups = lax.axis_size("fsdp")
    per_owner = experts // owners
    tok_rows = tokens.shape[0]
    bits, group_bits = masks("expert"), masks("fsdp")
    z_bits = bits[: len(bits) - len(low_bits("expert"))]
    me = lax.axis_index("expert").astype(jnp.int32).reshape(1)
    exponents = exponents.swapaxes(2, 3)

    half = bits[0]
    far, near = list(range(half, owners)), list(range(1, half))
    first, second, third, fourth = (far[i * half // 4 : (i + 1) * half // 4] for i in range(4))
    begin, rest = near[: (half - 1) // 3], near[(half - 1) // 3 :]
    late = rest + fourth

    def block(partner, learner_rows, exponents):
        return encode(
            learner_rows, exponents, me, partner, 0, per_owner, unit_rows, lambda m: 0
        )

    sent, arrived = {}, {}
    for d in first + second + third + begin:
        sent[d] = block(d, learner_rows, exponents)

    def after(value, keys, table):
        value, *blocks = together(value, *[table[key] for key in keys])
        table.update(zip(keys, blocks))
        return value

    def send(keys):
        for key in keys:
            arrived[key] = swap(sent[key], "expert", key)

    table = gather(share_table(expert_ids, route_probs, experts), "expert", z_bits[:1])
    held = gather(tokens, "expert", z_bits[:1])
    held = jnp.concatenate([held, table], axis=1)
    held = after(held, first + second, sent)
    send(first + second)
    held = gather(held, "expert", z_bits[1:])
    held = after(held, third + begin, sent)
    send(third + begin)

    def serve(held, learner_rows, exponents):
        makes = [functools.partial(block, d, learner_rows, exponents) for d in late]
        return layer(held, learner_rows, exponents, makes)

    def idle(held, learner_rows, exponents):
        out = jnp.zeros((groups, held.shape[0], width), jnp.float32)
        return out, *[block(d, learner_rows, exponents) for d in late]

    out, *blocks = lax.cond(
        expert_ids[0, 0] >= 0, serve, idle, held, learner_rows, exponents
    )
    sent.update(zip(late, blocks))
    out = after(out, first, arrived)

    out = out.reshape(groups, -1, tok_rows, width).swapaxes(0, 1)
    for bit, there in zip(reversed(z_bits), (second + begin, third, [], [])):
        out = halve(out, "expert", [bit])
        out = after(out, there, arrived)
    send(late)
    mixed = uncolumns(out.astype(jnp.bfloat16).reshape(groups * tok_rows, width), group_bits)

    elements = encode(
        learner_rows, exponents, me, 0, 0, per_owner, owners * unit_rows, lambda m: m
    )
    for key in first + second + begin + third + rest + fourth:
        elements = place(elements, arrived[key], me, key)
    return elements, mixed


def solution(mesh):
    return jax.shard_map(
        body,
        mesh=mesh,
        in_specs=(
            P(("fsdp", "expert"), None),
            P(None, None, "expert", "fsdp"),
            P(None, None, "expert", "fsdp"),
            P(("fsdp", "expert"), None),
            P(("fsdp", "expert"), None),
        ),
        out_specs=(P("expert", None, None, "fsdp"), P(("fsdp", "expert"), None)),
        check_vma=False,
    )
```

```python
import functools

import jax
import jax.numpy as jnp
from jax import lax
from jax.experimental import pallas as pl
from jax.experimental.pallas import tpu as pltpu
from jax.sharding import PartitionSpec as P

HALVES, ONES, TWOS = 1.5 * 2.0**22, 1.5 * 2.0**23, 1.5 * 2.0**24


def spread(values, width):
    blocks = values.shape[0]
    shape = (blocks, width)
    feature = lax.broadcasted_iota(jnp.int32, shape, 1)
    block = lax.broadcasted_iota(jnp.int32, shape, 0)
    size = width // blocks
    inside = (feature >= block * size) & (feature < (block + 1) * size)
    table = inside.astype(jnp.float32).astype(jnp.bfloat16)
    return lax.dot_general(
        values.astype(jnp.bfloat16),
        table,
        (((0,), (0,)), ((), ())),
        preferred_element_type=jnp.float32,
    )


def to_grid(rows, exponent):
    one = jnp.ones_like(exponent)
    inverse = lax.shift_left(one, -exponent).astype(jnp.float32)
    ratio = rows.astype(jnp.float32) * spread(inverse, rows.shape[1])
    ratio = jnp.clip(ratio, -6.0, 6.0)
    magnitude = jnp.abs(ratio)
    magic = jnp.where(magnitude < 2.0, HALVES, jnp.where(magnitude < 4.0, ONES, TWOS))
    return (ratio + magic) - magic


def encode_kernel(me, rows_ref, exponent_ref, out_ref):
    for part in range(rows_ref.shape[1]):
        value = to_grid(rows_ref[0, part], exponent_ref[0, part])
        out_ref[0, part] = value.astype(out_ref.dtype)


def encode(learner_rows, exponents, me, partner, first, count, out_rows, out_block):
    experts, parts, unit_rows, width = learner_rows.shape
    blocks = exponents.shape[2]
    per_owner = experts // lax.axis_size("expert")

    def place(i, s):
        return ((s[0] ^ partner) * per_owner + first + i, 0, 0, 0)

    return pl.pallas_call(
        encode_kernel,
        out_shape=jax.ShapeDtypeStruct((count, parts, out_rows, width), learner_rows.dtype),
        grid_spec=pltpu.PrefetchScalarGridSpec(
            num_scalar_prefetch=1,
            grid=(count,),
            in_specs=[
                pl.BlockSpec((1, parts, unit_rows, width), place),
                pl.BlockSpec((1, parts, blocks, unit_rows), place),
            ],
            out_specs=pl.BlockSpec(
                (1, parts, unit_rows, width), lambda i, s: (i, 0, out_block(s[0]), 0)
            ),
        ),
        cost_estimate=pl.CostEstimate(
            flops=20 * count * parts * unit_rows * width,
            bytes_accessed=4 * count * parts * unit_rows * width,
            transcendentals=0,
        ),
    )(me, learner_rows, exponents)


def weights_kernel(first, rows_ref, exponent_ref, out_ref):
    for part in range(out_ref.shape[0]):
        exponent = exponent_ref[0, part]
        value = to_grid(rows_ref[0, part], exponent)
        scale = jnp.exp2(exponent.astype(jnp.float32))
        out_ref[part, 0] = (value * spread(scale, value.shape[1])).astype(out_ref.dtype)


def dequantize(learner_rows, exponents, first, count):
    experts, parts, unit_rows, width = learner_rows.shape
    blocks = exponents.shape[2]
    size = count * experts * unit_rows * width
    return pl.pallas_call(
        functools.partial(weights_kernel, first),
        out_shape=jax.ShapeDtypeStruct((count, experts, unit_rows, width), learner_rows.dtype),
        grid=(experts,),
        in_specs=[
            pl.BlockSpec((1, count, unit_rows, width), lambda i: (i, first // count, 0, 0)),
            pl.BlockSpec((1, count, blocks, unit_rows), lambda i: (i, first // count, 0, 0)),
        ],
        out_specs=pl.BlockSpec((count, 1, unit_rows, width), lambda i: (0, i, 0, 0)),
        cost_estimate=pl.CostEstimate(
            flops=25 * size, bytes_accessed=4 * size, transcendentals=0
        ),
    )(learner_rows, exponents)


def place(elements, block, me, partner, first):
    row = (me[0] ^ partner) * block.shape[2]
    return lax.dynamic_update_slice(elements, block, (first, 0, row, 0))


def swap(value, axis, bit):
    return lax.ppermute(value, axis, [(i, i ^ bit) for i in range(lax.axis_size(axis))])


def together(*values):
    return lax.optimization_barrier(values)


def masks(axis):
    return [1 << b for b in reversed(range(lax.axis_size(axis).bit_length() - 1))]


def low_bits(axis):
    bits = masks(axis)
    return bits[len(bits) - len(bits) // 2 :]


def share_table(expert_ids, route_probs, experts):
    share = route_probs / jnp.sum(route_probs, axis=1, keepdims=True)
    named = expert_ids[:, :, None] == jnp.arange(experts, dtype=jnp.int32)[None, None, :]
    table = jnp.sum(jnp.where(named, share[:, :, None], 0.0), axis=1)
    pieces = []
    for _ in range(3):
        piece = lax.reduce_precision(table, 8, 7)
        table = table - piece
        pieces.append(piece.astype(jnp.bfloat16))
    pieces = jnp.concatenate(pieces, axis=1)
    return jnp.pad(pieces, ((0, 0), (0, -pieces.shape[1] % 128)))


def gather(value, axis, bits):
    for bit in bits:
        value = jnp.concatenate([value, swap(value, axis, bit)], axis=0)
    return value


def halve(value, axis, bits):
    for bit in reversed(bits):
        kept = value.shape[0] // 2
        got = swap(value[kept:].astype(jnp.bfloat16), axis, bit)
        value = value[:kept].astype(jnp.float32) + got.astype(jnp.float32)
    return value


def columns(value, bits):
    group = lax.axis_index("fsdp")
    for bit in bits:
        kept = value.shape[1] // 2
        low, high = value[:, :kept], value[:, kept:]
        upper = (group & bit) != 0
        mine, other = jnp.where(upper, high, low), jnp.where(upper, low, high)
        value = jnp.concatenate([mine, swap(other, "fsdp", bit)], axis=0)
    return value


def uncolumns(value, bits):
    group = lax.axis_index("fsdp")
    for bit in reversed(bits):
        kept = value.shape[0] // 2
        mine, other = value[:kept], swap(value[kept:], "fsdp", bit)
        upper = (group & bit) != 0
        value = jnp.concatenate(
            [jnp.where(upper, other, mine), jnp.where(upper, mine, other)], axis=1
        )
    return value


def layer(held, learner_rows, exponents, encode_more):
    experts, parts, unit_rows, width = learner_rows.shape
    groups = lax.axis_size("fsdp")
    x_bits, group_bits = low_bits("expert"), masks("fsdp")
    units = experts * unit_rows
    rows = held.shape[0]
    slots = rows << len(x_bits)

    table = held[:, groups * width :]
    held = columns(held[:, : groups * width], group_bits).reshape(groups, rows, width)
    pair = dequantize(learner_rows, exponents, 0, 2)
    for bit in x_bits:
        held = jnp.concatenate([held, swap(held, "expert", bit)], axis=1)
    held, pair, table = together(held, pair, table)
    table = gather(table, "expert", x_bits)
    partial = lax.dot_general(
        held.reshape(groups * slots, width),
        pair.reshape(-1, width),
        (((1,), (1,)), ((), ())),
        preferred_element_type=jnp.float32,
    ).astype(jnp.bfloat16)
    partial, table = together(partial, table)
    table = table[:, : 3 * experts].astype(jnp.float32).reshape(-1, 3, experts).sum(axis=1)

    down = dequantize(learner_rows, exponents, 2, 1)
    partial = halve(partial, "fsdp", group_bits)
    partial, down = together(partial, down)
    hidden = jax.nn.silu(partial[:, :units]) * partial[:, units:]
    shared = hidden.reshape(-1, experts, unit_rows) * table[:, :, None]
    shared = shared.astype(jnp.bfloat16).reshape(-1, units)
    middle = len(encode_more) // 2
    more = [make() for make in encode_more]
    shared, *first = together(gather(shared, "fsdp", group_bits), *more[:middle])
    out = jnp.dot(shared, down.reshape(-1, width), preferred_element_type=jnp.float32)
    out = out.reshape(groups, slots, width)
    for bit in reversed(x_bits):
        kept = out.shape[1] // 2
        out = out[:, :kept] + swap(out[:, kept:].astype(jnp.bfloat16), "expert", bit)
    out, *second = together(out, *more[middle:])
    return out, *first, *second


def body(tokens, learner_rows, exponents, expert_ids, route_probs):
    experts, parts, unit_rows, width = learner_rows.shape
    owners = lax.axis_size("expert")
    groups = lax.axis_size("fsdp")
    per_owner = experts // owners
    tok_rows = tokens.shape[0]
    bits, group_bits = masks("expert"), masks("fsdp")
    z_bits = bits[: len(bits) - len(low_bits("expert"))]
    me = lax.axis_index("expert").astype(jnp.int32).reshape(1)
    exponents = exponents.swapaxes(2, 3)

    half, low = bits[0], low_bits("expert")[0] * 2
    far = [(d, 0, per_owner) for d in sorted(range(half, owners), key=lambda d: d % low)]
    first, second, third, fourth = (far[i * half // 4 : (i + 1) * half // 4] for i in range(4))
    begin = [(d, 0, per_owner) for d in range(low, half) if d % low]
    rest = [(d, 0, per_owner) for d in range(1, half) if d < low or not d % low]
    fourth = [(d, k, 1) for k in range(per_owner) for d, _, _ in fourth]
    soon, late = fourth[: half // 4], fourth[half // 4 :]

    def block(key, learner_rows, exponents):
        return encode(learner_rows, exponents, me, *key, unit_rows, lambda m: 0)

    sent, arrived = {}, {}
    for key in first + second + third + begin:
        sent[key] = block(key, learner_rows, exponents)

    def after(value, keys, table):
        value, *blocks = together(value, *[table[key] for key in keys])
        table.update(zip(keys, blocks))
        return value

    def send(keys):
        for key in keys:
            arrived[key] = swap(sent[key], "expert", key[0])

    table = gather(share_table(expert_ids, route_probs, experts), "expert", z_bits[:1])
    held = after(tokens, first, sent)
    held = gather(held, "expert", z_bits[:1])
    held = after(held, second, sent)
    held = jnp.concatenate([held, table], axis=1)
    held = gather(held, "expert", z_bits[1:])
    held = after(held, third + begin, sent)
    send(first + second + third + begin)

    def serve(held, learner_rows, exponents):
        makes = [functools.partial(block, d, learner_rows, exponents) for d in soon + late + rest]
        return layer(held, learner_rows, exponents, makes)

    def idle(held, learner_rows, exponents):
        out = jnp.zeros((groups, held.shape[0], width), jnp.float32)
        return out, *[block(d, learner_rows, exponents) for d in soon + late + rest]

    out, *blocks = lax.cond(
        expert_ids[0, 0] >= 0, serve, idle, held, learner_rows, exponents
    )
    sent.update(zip(soon + late + rest, blocks))
    out = after(out, first, arrived)

    out = out.reshape(groups, -1, tok_rows, width).swapaxes(0, 1)
    out = halve(out, "expert", z_bits[1:])
    out = after(out, second + begin, arrived)
    out = after(out, soon + rest, sent)
    send(soon + rest)
    out = halve(out, "expert", z_bits[:1])
    out = after(out, third, arrived)
    out = after(out, late, sent)
    send(late)
    mixed = uncolumns(out.astype(jnp.bfloat16).reshape(groups * tok_rows, width), group_bits)

    elements = encode(
        learner_rows, exponents, me, 0, 0, per_owner, owners * unit_rows, lambda m: m
    )
    for key in first + second + begin + third + rest + soon + late:
        elements = place(elements, arrived[key], me, *key[:2])
    return elements, mixed


def solution(mesh):
    return jax.shard_map(
        body,
        mesh=mesh,
        in_specs=(
            P(("fsdp", "expert"), None),
            P(None, None, "expert", "fsdp"),
            P(None, None, "expert", "fsdp"),
            P(("fsdp", "expert"), None),
            P(("fsdp", "expert"), None),
        ),
        out_specs=(P("expert", None, None, "fsdp"), P(("fsdp", "expert"), None)),
        check_vma=False,
    )
```

```python
import functools

import jax
import jax.numpy as jnp
from jax import lax
from jax.experimental import pallas as pl
from jax.experimental.pallas import tpu as pltpu
from jax.sharding import PartitionSpec as P

HALVES, ONES, TWOS = 1.5 * 2.0**22, 1.5 * 2.0**23, 1.5 * 2.0**24


def spread(values, width):
    blocks = values.shape[0]
    shape = (blocks, width)
    feature = lax.broadcasted_iota(jnp.int32, shape, 1)
    block = lax.broadcasted_iota(jnp.int32, shape, 0)
    size = width // blocks
    inside = (feature >= block * size) & (feature < (block + 1) * size)
    table = inside.astype(jnp.float32).astype(jnp.bfloat16)
    return lax.dot_general(
        values.astype(jnp.bfloat16),
        table,
        (((0,), (0,)), ((), ())),
        preferred_element_type=jnp.float32,
    )


def to_grid(rows, exponent):
    one = jnp.ones_like(exponent)
    inverse = lax.shift_left(one, -exponent).astype(jnp.float32)
    ratio = rows.astype(jnp.float32) * spread(inverse, rows.shape[1])
    ratio = jnp.clip(ratio, -6.0, 6.0)
    magnitude = jnp.abs(ratio)
    magic = jnp.where(magnitude < 2.0, HALVES, jnp.where(magnitude < 4.0, ONES, TWOS))
    return (ratio + magic) - magic


def encode_kernel(me, rows_ref, exponent_ref, out_ref):
    for part in range(rows_ref.shape[1]):
        value = to_grid(rows_ref[0, part], exponent_ref[0, part])
        out_ref[0, part] = value.astype(out_ref.dtype)


def encode(learner_rows, exponents, me, partner, out_rows, out_block):
    experts, parts, unit_rows, width = learner_rows.shape
    blocks = exponents.shape[2]
    per_owner = experts // lax.axis_size("expert")

    def expert(i, s):
        return ((s[0] ^ partner) * per_owner + i, 0, 0, 0)

    value = pl.pallas_call(
        encode_kernel,
        out_shape=jax.ShapeDtypeStruct((per_owner, parts, out_rows, width), learner_rows.dtype),
        grid_spec=pltpu.PrefetchScalarGridSpec(
            num_scalar_prefetch=1,
            grid=(per_owner,),
            in_specs=[
                pl.BlockSpec((1, parts, unit_rows, width), expert),
                pl.BlockSpec((1, parts, blocks, unit_rows), expert),
            ],
            out_specs=pl.BlockSpec(
                (1, parts, unit_rows, width), lambda i, s: (i, 0, out_block(s[0]), 0)
            ),
        ),
        cost_estimate=pl.CostEstimate(
            flops=20 * per_owner * parts * unit_rows * width,
            bytes_accessed=4 * per_owner * parts * unit_rows * width,
            transcendentals=0,
        ),
    )(me, learner_rows, exponents)
    return value.reshape(per_owner * parts, out_rows, width)


def weights_kernel(first, rows_ref, exponent_ref, out_ref):
    for part in range(out_ref.shape[0]):
        exponent = exponent_ref[0, part]
        value = to_grid(rows_ref[0, part], exponent)
        scale = jnp.exp2(exponent.astype(jnp.float32))
        out_ref[part, 0] = (value * spread(scale, value.shape[1])).astype(out_ref.dtype)


def dequantize(learner_rows, exponents, first, count):
    experts, parts, unit_rows, width = learner_rows.shape
    blocks = exponents.shape[2]
    size = count * experts * unit_rows * width
    return pl.pallas_call(
        functools.partial(weights_kernel, first),
        out_shape=jax.ShapeDtypeStruct((count, experts, unit_rows, width), learner_rows.dtype),
        grid=(experts,),
        in_specs=[
            pl.BlockSpec((1, count, unit_rows, width), lambda i: (i, first // count, 0, 0)),
            pl.BlockSpec((1, count, blocks, unit_rows), lambda i: (i, first // count, 0, 0)),
        ],
        out_specs=pl.BlockSpec((count, 1, unit_rows, width), lambda i: (0, i, 0, 0)),
        cost_estimate=pl.CostEstimate(
            flops=25 * size, bytes_accessed=4 * size, transcendentals=0
        ),
    )(learner_rows, exponents)


def place(elements, block, me, partner):
    return lax.dynamic_update_slice(elements, block, (0, (me[0] ^ partner) * block.shape[1], 0))


def swap(value, axis, bit):
    return lax.ppermute(value, axis, [(i, i ^ bit) for i in range(lax.axis_size(axis))])


def together(*values):
    return lax.optimization_barrier(values)


def masks(axis):
    return [1 << b for b in reversed(range(lax.axis_size(axis).bit_length() - 1))]


def low_bits(axis):
    bits = masks(axis)
    return bits[len(bits) - len(bits) // 2 :]


def share_table(expert_ids, route_probs, experts):
    share = route_probs / jnp.sum(route_probs, axis=1, keepdims=True)
    named = expert_ids[:, :, None] == jnp.arange(experts, dtype=jnp.int32)[None, None, :]
    table = jnp.sum(jnp.where(named, share[:, :, None], 0.0), axis=1)
    pieces = []
    for _ in range(3):
        piece = lax.reduce_precision(table, 8, 7)
        table = table - piece
        pieces.append(piece.astype(jnp.bfloat16))
    pieces = jnp.concatenate(pieces, axis=1)
    return jnp.pad(pieces, ((0, 0), (0, -pieces.shape[1] % 128)))


def gather(value, axis, bits):
    for bit in bits:
        value = jnp.concatenate([value, swap(value, axis, bit)], axis=0)
    return value


def halve(value, axis, bits):
    for bit in reversed(bits):
        kept = value.shape[0] // 2
        got = swap(value[kept:].astype(jnp.bfloat16), axis, bit)
        value = value[:kept].astype(jnp.float32) + got.astype(jnp.float32)
    return value


def columns(value, bits):
    group = lax.axis_index("fsdp")
    for bit in bits:
        kept = value.shape[1] // 2
        low, high = value[:, :kept], value[:, kept:]
        upper = (group & bit) != 0
        mine, other = jnp.where(upper, high, low), jnp.where(upper, low, high)
        value = jnp.concatenate([mine, swap(other, "fsdp", bit)], axis=0)
    return value


def uncolumns(value, bits):
    group = lax.axis_index("fsdp")
    for bit in reversed(bits):
        kept = value.shape[0] // 2
        mine, other = value[:kept], swap(value[kept:], "fsdp", bit)
        upper = (group & bit) != 0
        value = jnp.concatenate(
            [jnp.where(upper, other, mine), jnp.where(upper, mine, other)], axis=1
        )
    return value


def layer(held, learner_rows, exponents, encode_more):
    experts, parts, unit_rows, width = learner_rows.shape
    groups = lax.axis_size("fsdp")
    x_bits, group_bits = low_bits("expert"), masks("fsdp")
    units = experts * unit_rows
    rows = held.shape[0]
    slots = rows << len(x_bits)

    table = held[:, groups * width :]
    held = columns(held[:, : groups * width], group_bits).reshape(groups, rows, width)
    pair = dequantize(learner_rows, exponents, 0, 2)

    def swap_all(values, bit):
        rows = [value.reshape(-1, width) for value in values]
        got = swap(jnp.concatenate(rows, axis=0), "expert", bit)
        ends = [sum(part.shape[0] for part in rows[:i]) for i in range(len(rows) + 1)]
        return [
            got[start:end].reshape(value.shape)
            for start, end, value in zip(ends, ends[1:], values)
        ]

    for bit in x_bits:
        got, got_table = swap_all([held, table], bit)
        held = jnp.concatenate([held, got], axis=1)
        table = jnp.concatenate([table, got_table], axis=0)
    held, pair, table = together(held, pair, table)
    partial = lax.dot_general(
        held.reshape(groups * slots, width),
        pair.reshape(-1, width),
        (((1,), (1,)), ((), ())),
        preferred_element_type=jnp.float32,
    ).astype(jnp.bfloat16)
    partial, table = together(partial, table)
    table = table[:, : 3 * experts].astype(jnp.float32).reshape(-1, 3, experts).sum(axis=1)

    down = dequantize(learner_rows, exponents, 2, 1)
    partial = halve(partial, "fsdp", group_bits)
    partial, down = together(partial, down)
    hidden = jax.nn.silu(partial[:, :units]) * partial[:, units:]
    shared = hidden.reshape(-1, experts, unit_rows) * table[:, :, None]
    shared = shared.astype(jnp.bfloat16).reshape(-1, units)
    shared, *more = together(gather(shared, "fsdp", group_bits), *encode_more())
    out = jnp.dot(shared, down.reshape(-1, width), preferred_element_type=jnp.float32)
    out = out.reshape(groups, slots, width)
    for bit in reversed(x_bits):
        kept = out.shape[1] // 2
        out = out[:, :kept] + swap(out[:, kept:].astype(jnp.bfloat16), "expert", bit)
    return out, *more


def body(tokens, learner_rows, exponents, expert_ids, route_probs):
    experts, parts, unit_rows, width = learner_rows.shape
    owners = lax.axis_size("expert")
    groups = lax.axis_size("fsdp")
    per_owner = experts // owners
    tok_rows = tokens.shape[0]
    bits, group_bits = masks("expert"), masks("fsdp")
    z_bits = bits[: len(bits) - len(low_bits("expert"))]
    me = lax.axis_index("expert").astype(jnp.int32).reshape(1)
    exponents = exponents.swapaxes(2, 3)

    half, low = bits[0], low_bits("expert")[0] * 2
    straight = list(range(half, owners, low))
    turning = [d for d in range(half, owners) if d % low]
    far = turning[: half // 4] + straight + turning[half // 4 :]
    first, second, third, fourth = (far[i * half // 4 : (i + 1) * half // 4] for i in range(4))
    begin = [d for d in range(low, half) if d % low]
    late = fourth + [d for d in range(1, half) if d not in begin]

    def blocks(partners, learner_rows, exponents):
        unit_rows = learner_rows.shape[2]
        return [
            encode(learner_rows, exponents, me, d, unit_rows, lambda m: 0) for d in partners
        ]

    early = first + second + third + begin
    sent, arrived = dict(zip(early, blocks(early, learner_rows, exponents))), {}

    def after(value, keys, table):
        value, *blocks = together(value, *[table[key] for key in keys])
        table.update(zip(keys, blocks))
        return value

    def send(keys):
        for key in keys:
            arrived[key] = swap(sent[key], "expert", key)

    table = gather(share_table(expert_ids, route_probs, experts), "expert", z_bits[:1])
    held = after(tokens, first, sent)
    held = gather(held, "expert", z_bits[:1])
    held = after(held, second, sent)
    held = jnp.concatenate([held, table], axis=1)
    held = gather(held, "expert", z_bits[1:])
    held = after(held, third + begin, sent)
    send(early)

    def serve(held, learner_rows, exponents):
        return layer(
            held, learner_rows, exponents, lambda: blocks(late, learner_rows, exponents)
        )

    def idle(held, learner_rows, exponents):
        out = jnp.zeros((groups, held.shape[0], width), jnp.float32)
        return out, *blocks(late, learner_rows, exponents)

    out, *got = lax.cond(expert_ids[0, 0] >= 0, serve, idle, held, learner_rows, exponents)
    sent.update(zip(late, got))
    out = after(out, first, arrived)

    out = out.reshape(groups, -1, tok_rows, width).swapaxes(0, 1)
    out = halve(out, "expert", z_bits[1:])
    out = after(out, second + begin, arrived)
    out = after(out, late, sent)
    send(late)
    out = halve(out, "expert", z_bits[:1])
    out = after(out, third, arrived)
    mixed = uncolumns(out.astype(jnp.bfloat16).reshape(groups * tok_rows, width), group_bits)

    elements = encode(learner_rows, exponents, me, 0, owners * unit_rows, lambda m: m)
    for partner in first + second + begin + third + late[len(fourth) :] + fourth:
        elements = place(elements, arrived[partner], me, partner)
    return elements.reshape(per_owner, parts, owners * unit_rows, width), mixed


def solution(mesh):
    return jax.shard_map(
        body,
        mesh=mesh,
        in_specs=(
            P(("fsdp", "expert"), None),
            P(None, None, "expert", "fsdp"),
            P(None, None, "expert", "fsdp"),
            P(("fsdp", "expert"), None),
            P(("fsdp", "expert"), None),
        ),
        out_specs=(P("expert", None, None, "fsdp"), P(("fsdp", "expert"), None)),
        check_vma=False,
    )
```

```python
import functools

import jax
import jax.numpy as jnp
from jax import lax
from jax.experimental import pallas as pl
from jax.experimental.pallas import tpu as pltpu
from jax.sharding import PartitionSpec as P

HALVES, ONES, TWOS = 1.5 * 2.0**22, 1.5 * 2.0**23, 1.5 * 2.0**24


def spread(values, width):
    blocks = values.shape[0]
    shape = (blocks, width)
    feature = lax.broadcasted_iota(jnp.int32, shape, 1)
    block = lax.broadcasted_iota(jnp.int32, shape, 0)
    size = width // blocks
    inside = (feature >= block * size) & (feature < (block + 1) * size)
    table = inside.astype(jnp.float32).astype(jnp.bfloat16)
    return lax.dot_general(
        values.astype(jnp.bfloat16),
        table,
        (((0,), (0,)), ((), ())),
        preferred_element_type=jnp.float32,
    )


def to_grid(rows, exponent):
    one = jnp.ones_like(exponent)
    inverse = lax.shift_left(one, -exponent).astype(jnp.float32)
    ratio = rows.astype(jnp.float32) * spread(inverse, rows.shape[1])
    ratio = jnp.clip(ratio, -6.0, 6.0)
    magnitude = jnp.abs(ratio)
    magic = jnp.where(magnitude < 2.0, HALVES, jnp.where(magnitude < 4.0, ONES, TWOS))
    return (ratio + magic) - magic


def encode_kernel(me, rows_ref, exponent_ref, out_ref):
    for part in range(rows_ref.shape[1]):
        value = to_grid(rows_ref[0, part], exponent_ref[0, part])
        out_ref[0, part] = value.astype(out_ref.dtype)


def encode(learner_rows, exponents, me, partner, out_rows, out_block):
    experts, parts, unit_rows, width = learner_rows.shape
    blocks = exponents.shape[2]
    per_owner = experts // lax.axis_size("expert")

    def expert(i, s):
        return ((s[0] ^ partner) * per_owner + i, 0, 0, 0)

    value = pl.pallas_call(
        encode_kernel,
        out_shape=jax.ShapeDtypeStruct((per_owner, parts, out_rows, width), learner_rows.dtype),
        grid_spec=pltpu.PrefetchScalarGridSpec(
            num_scalar_prefetch=1,
            grid=(per_owner,),
            in_specs=[
                pl.BlockSpec((1, parts, unit_rows, width), expert),
                pl.BlockSpec((1, parts, blocks, unit_rows), expert),
            ],
            out_specs=pl.BlockSpec(
                (1, parts, unit_rows, width), lambda i, s: (i, 0, out_block(s[0]), 0)
            ),
        ),
        cost_estimate=pl.CostEstimate(
            flops=20 * per_owner * parts * unit_rows * width,
            bytes_accessed=4 * per_owner * parts * unit_rows * width,
            transcendentals=0,
        ),
    )(me, learner_rows, exponents)
    return value.reshape(per_owner * parts, out_rows, width)


def weights_kernel(first, rows_ref, exponent_ref, out_ref):
    for part in range(out_ref.shape[0]):
        exponent = exponent_ref[0, part]
        value = to_grid(rows_ref[0, part], exponent)
        scale = jnp.exp2(exponent.astype(jnp.float32))
        out_ref[part, 0] = (value * spread(scale, value.shape[1])).astype(out_ref.dtype)


def dequantize(learner_rows, exponents, first, count):
    experts, parts, unit_rows, width = learner_rows.shape
    blocks = exponents.shape[2]
    size = count * experts * unit_rows * width
    return pl.pallas_call(
        functools.partial(weights_kernel, first),
        out_shape=jax.ShapeDtypeStruct((count, experts, unit_rows, width), learner_rows.dtype),
        grid=(experts,),
        in_specs=[
            pl.BlockSpec((1, count, unit_rows, width), lambda i: (i, first // count, 0, 0)),
            pl.BlockSpec((1, count, blocks, unit_rows), lambda i: (i, first // count, 0, 0)),
        ],
        out_specs=pl.BlockSpec((count, 1, unit_rows, width), lambda i: (0, i, 0, 0)),
        cost_estimate=pl.CostEstimate(
            flops=25 * size, bytes_accessed=4 * size, transcendentals=0
        ),
    )(learner_rows, exponents)


def place(elements, block, me, partner):
    return lax.dynamic_update_slice(elements, block, (0, (me[0] ^ partner) * block.shape[1], 0))


def swap(value, axis, bit):
    return lax.ppermute(value, axis, [(i, i ^ bit) for i in range(lax.axis_size(axis))])


def together(*values):
    return lax.optimization_barrier(values)


def masks(axis):
    return [1 << b for b in reversed(range(lax.axis_size(axis).bit_length() - 1))]


def low_bits(axis):
    bits = masks(axis)
    return bits[len(bits) - len(bits) // 2 :]


def share_table(expert_ids, route_probs, experts):
    share = route_probs / jnp.sum(route_probs, axis=1, keepdims=True)
    named = expert_ids[:, :, None] == jnp.arange(experts, dtype=jnp.int32)[None, None, :]
    table = jnp.sum(jnp.where(named, share[:, :, None], 0.0), axis=1)
    pieces = []
    for _ in range(3):
        piece = lax.reduce_precision(table, 8, 7)
        table = table - piece
        pieces.append(piece.astype(jnp.bfloat16))
    pieces = jnp.concatenate(pieces, axis=1)
    return jnp.pad(pieces, ((0, 0), (0, -pieces.shape[1] % 128)))


def gather(value, axis, bits):
    for bit in bits:
        value = jnp.concatenate([value, swap(value, axis, bit)], axis=0)
    return value


def halve(value, axis, bits):
    for bit in reversed(bits):
        kept = value.shape[0] // 2
        got = swap(value[kept:].astype(jnp.bfloat16), axis, bit)
        value = value[:kept].astype(jnp.float32) + got.astype(jnp.float32)
    return value


def columns(value, bits):
    group = lax.axis_index("fsdp")
    for bit in bits:
        kept = value.shape[1] // 2
        low, high = value[:, :kept], value[:, kept:]
        upper = (group & bit) != 0
        mine, other = jnp.where(upper, high, low), jnp.where(upper, low, high)
        value = jnp.concatenate([mine, swap(other, "fsdp", bit)], axis=0)
    return value


def uncolumns(value, bits):
    group = lax.axis_index("fsdp")
    for bit in reversed(bits):
        kept = value.shape[0] // 2
        mine, other = value[:kept], swap(value[kept:], "fsdp", bit)
        upper = (group & bit) != 0
        value = jnp.concatenate(
            [jnp.where(upper, other, mine), jnp.where(upper, mine, other)], axis=1
        )
    return value


def layer(held, learner_rows, exponents, encode_more):
    experts, parts, unit_rows, width = learner_rows.shape
    groups = lax.axis_size("fsdp")
    x_bits, group_bits = low_bits("expert"), masks("fsdp")
    units = experts * unit_rows
    rows = held.shape[0]
    slots = rows << len(x_bits)

    table = held[:, groups * width :]
    held = columns(held[:, : groups * width], group_bits).reshape(groups, rows, width)
    pair = dequantize(learner_rows, exponents, 0, 2)

    def swap_all(values, bit):
        rows = [value.reshape(-1, width) for value in values]
        got = swap(jnp.concatenate(rows, axis=0), "expert", bit)
        ends = [sum(part.shape[0] for part in rows[:i]) for i in range(len(rows) + 1)]
        return [
            got[start:end].reshape(value.shape)
            for start, end, value in zip(ends, ends[1:], values)
        ]

    for bit in x_bits:
        got, got_table = swap_all([held, table], bit)
        held = jnp.concatenate([held, got], axis=1)
        table = jnp.concatenate([table, got_table], axis=0)
    held, pair, table = together(held, pair, table)
    partial = lax.dot_general(
        held.reshape(groups * slots, width),
        pair.reshape(-1, width),
        (((1,), (1,)), ((), ())),
        preferred_element_type=jnp.float32,
    ).astype(jnp.bfloat16)
    partial, table = together(partial, table)
    table = table[:, : 3 * experts].astype(jnp.float32).reshape(-1, 3, experts).sum(axis=1)

    down = dequantize(learner_rows, exponents, 2, 1)
    partial = halve(partial, "fsdp", group_bits)
    partial, down = together(partial, down)
    hidden = jax.nn.silu(partial[:, :units]) * partial[:, units:]
    shared = hidden.reshape(-1, experts, unit_rows) * table[:, :, None]
    shared = shared.astype(jnp.bfloat16).reshape(-1, units)
    shared, *more = together(gather(shared, "fsdp", group_bits), *encode_more())
    out = jnp.dot(shared, down.reshape(-1, width), preferred_element_type=jnp.float32)
    out = out.reshape(groups, slots, width)
    for bit in reversed(x_bits):
        kept = out.shape[1] // 2
        out = out[:, :kept] + swap(out[:, kept:].astype(jnp.bfloat16), "expert", bit)
    return out, *more


def body(tokens, learner_rows, exponents, expert_ids, route_probs):
    experts, parts, unit_rows, width = learner_rows.shape
    owners = lax.axis_size("expert")
    groups = lax.axis_size("fsdp")
    per_owner = experts // owners
    tok_rows = tokens.shape[0]
    bits, group_bits = masks("expert"), masks("fsdp")
    z_bits = bits[: len(bits) - len(low_bits("expert"))]
    me = lax.axis_index("expert").astype(jnp.int32).reshape(1)
    exponents = exponents.swapaxes(2, 3)

    half, low = bits[0], low_bits("expert")[0] * 2
    straight = list(range(half, owners, low))
    turning = [d for d in range(half, owners) if d % low]
    far = turning[: half // 4] + straight + turning[half // 4 :]
    first, second, third, fourth = (far[i * half // 4 : (i + 1) * half // 4] for i in range(4))
    begin = [d for d in range(low, half) if d % low]
    late = fourth + [d for d in range(1, half) if d not in begin]

    def blocks(partners, learner_rows, exponents):
        unit_rows = learner_rows.shape[2]
        return [
            encode(learner_rows, exponents, me, d, unit_rows, lambda m: 0) for d in partners
        ]

    early = first + second + third + begin
    sent, arrived = dict(zip(early, blocks(early, learner_rows, exponents))), {}

    def after(value, keys, table):
        value, *blocks = together(value, *[table[key] for key in keys])
        table.update(zip(keys, blocks))
        return value

    def send(keys):
        for key in keys:
            arrived[key] = swap(sent[key], "expert", key)

    table = after(share_table(expert_ids, route_probs, experts), first, sent)
    table = gather(table, "expert", z_bits[:1])
    held = gather(tokens, "expert", z_bits[:1])
    held = after(held, second, sent)
    held = jnp.concatenate([held, table], axis=1)
    held = gather(held, "expert", z_bits[1:])
    held = after(held, third + begin, sent)
    send(early)

    def serve(held, learner_rows, exponents):
        return layer(
            held, learner_rows, exponents, lambda: blocks(late, learner_rows, exponents)
        )

    def idle(held, learner_rows, exponents):
        out = jnp.zeros((groups, held.shape[0], width), jnp.float32)
        return out, *blocks(late, learner_rows, exponents)

    out, *got = lax.cond(expert_ids[0, 0] >= 0, serve, idle, held, learner_rows, exponents)
    sent.update(zip(late, got))
    out = after(out, first, arrived)

    out = out.reshape(groups, -1, tok_rows, width).swapaxes(0, 1)
    out = halve(out, "expert", z_bits[1:])
    out = after(out, second + begin, arrived)
    out = after(out, late, sent)
    send(late)
    out = halve(out, "expert", z_bits[:1])
    out = after(out, third, arrived)
    mixed = uncolumns(out.astype(jnp.bfloat16).reshape(groups * tok_rows, width), group_bits)

    elements = encode(learner_rows, exponents, me, 0, owners * unit_rows, lambda m: m)
    for partner in first + second + begin + third + late[len(fourth) :] + fourth:
        elements = place(elements, arrived[partner], me, partner)
    return elements.reshape(per_owner, parts, owners * unit_rows, width), mixed


def solution(mesh):
    return jax.shard_map(
        body,
        mesh=mesh,
        in_specs=(
            P(("fsdp", "expert"), None),
            P(None, None, "expert", "fsdp"),
            P(None, None, "expert", "fsdp"),
            P(("fsdp", "expert"), None),
            P(("fsdp", "expert"), None),
        ),
        out_specs=(P("expert", None, None, "fsdp"), P(("fsdp", "expert"), None)),
        check_vma=False,
    )
```

```python
import functools

import jax
import jax.numpy as jnp
from jax import lax
from jax.experimental import pallas as pl
from jax.experimental.pallas import tpu as pltpu
from jax.sharding import PartitionSpec as P

HALVES, ONES, TWOS = 1.5 * 2.0**22, 1.5 * 2.0**23, 1.5 * 2.0**24


def spread(values, width):
    blocks = values.shape[0]
    shape = (blocks, width)
    feature = lax.broadcasted_iota(jnp.int32, shape, 1)
    block = lax.broadcasted_iota(jnp.int32, shape, 0)
    size = width // blocks
    inside = (feature >= block * size) & (feature < (block + 1) * size)
    table = inside.astype(jnp.float32).astype(jnp.bfloat16)
    return lax.dot_general(
        values.astype(jnp.bfloat16),
        table,
        (((0,), (0,)), ((), ())),
        preferred_element_type=jnp.float32,
    )


def to_grid(rows, exponent):
    one = jnp.ones_like(exponent)
    inverse = lax.shift_left(one, -exponent).astype(jnp.float32)
    ratio = rows.astype(jnp.float32) * spread(inverse, rows.shape[1])
    ratio = jnp.clip(ratio, -6.0, 6.0)
    magnitude = jnp.abs(ratio)
    magic = jnp.where(magnitude < 2.0, HALVES, jnp.where(magnitude < 4.0, ONES, TWOS))
    return (ratio + magic) - magic


def encode_kernel(me, rows_ref, exponent_ref, out_ref):
    for part in range(rows_ref.shape[1]):
        value = to_grid(rows_ref[0, part], exponent_ref[0, part])
        out_ref[0, part] = value.astype(out_ref.dtype)


def encode(learner_rows, exponents, me, partner, out_rows, out_block):
    experts, parts, unit_rows, width = learner_rows.shape
    blocks = exponents.shape[2]
    per_owner = experts // lax.axis_size("expert")

    def expert(i, s):
        return ((s[0] ^ partner) * per_owner + i, 0, 0, 0)

    value = pl.pallas_call(
        encode_kernel,
        out_shape=jax.ShapeDtypeStruct((per_owner, parts, out_rows, width), learner_rows.dtype),
        grid_spec=pltpu.PrefetchScalarGridSpec(
            num_scalar_prefetch=1,
            grid=(per_owner,),
            in_specs=[
                pl.BlockSpec((1, parts, unit_rows, width), expert),
                pl.BlockSpec((1, parts, blocks, unit_rows), expert),
            ],
            out_specs=pl.BlockSpec(
                (1, parts, unit_rows, width), lambda i, s: (i, 0, out_block(s[0]), 0)
            ),
        ),
        cost_estimate=pl.CostEstimate(
            flops=20 * per_owner * parts * unit_rows * width,
            bytes_accessed=4 * per_owner * parts * unit_rows * width,
            transcendentals=0,
        ),
    )(me, learner_rows, exponents)
    return value.reshape(per_owner * parts, out_rows, width)


def weights_kernel(first, rows_ref, exponent_ref, out_ref):
    for part in range(out_ref.shape[0]):
        exponent = exponent_ref[0, part]
        value = to_grid(rows_ref[0, part], exponent)
        scale = jnp.exp2(exponent.astype(jnp.float32))
        out_ref[part, 0] = (value * spread(scale, value.shape[1])).astype(out_ref.dtype)


def dequantize(learner_rows, exponents, first, count):
    experts, parts, unit_rows, width = learner_rows.shape
    blocks = exponents.shape[2]
    size = count * experts * unit_rows * width
    return pl.pallas_call(
        functools.partial(weights_kernel, first),
        out_shape=jax.ShapeDtypeStruct((count, experts, unit_rows, width), learner_rows.dtype),
        grid=(experts,),
        in_specs=[
            pl.BlockSpec((1, count, unit_rows, width), lambda i: (i, first // count, 0, 0)),
            pl.BlockSpec((1, count, blocks, unit_rows), lambda i: (i, first // count, 0, 0)),
        ],
        out_specs=pl.BlockSpec((count, 1, unit_rows, width), lambda i: (0, i, 0, 0)),
        cost_estimate=pl.CostEstimate(
            flops=25 * size, bytes_accessed=4 * size, transcendentals=0
        ),
    )(learner_rows, exponents)


def place(elements, block, me, partner):
    return lax.dynamic_update_slice(elements, block, (0, (me[0] ^ partner) * block.shape[1], 0))


def swap(value, axis, bit):
    return lax.ppermute(value, axis, [(i, i ^ bit) for i in range(lax.axis_size(axis))])


def together(*values):
    return lax.optimization_barrier(values)


def masks(axis):
    return [1 << b for b in reversed(range(lax.axis_size(axis).bit_length() - 1))]


def low_bits(axis):
    bits = masks(axis)
    return bits[len(bits) - len(bits) // 2 :]


def share_table(expert_ids, route_probs, experts):
    share = route_probs / jnp.sum(route_probs, axis=1, keepdims=True)
    named = expert_ids[:, :, None] == jnp.arange(experts, dtype=jnp.int32)[None, None, :]
    table = jnp.sum(jnp.where(named, share[:, :, None], 0.0), axis=1)
    pieces = []
    for _ in range(3):
        piece = lax.reduce_precision(table, 8, 7)
        table = table - piece
        pieces.append(piece.astype(jnp.bfloat16))
    pieces = jnp.concatenate(pieces, axis=1)
    return jnp.pad(pieces, ((0, 0), (0, -pieces.shape[1] % 128)))


def gather(value, axis, bits):
    for bit in bits:
        value = jnp.concatenate([value, swap(value, axis, bit)], axis=0)
    return value


def halve(value, axis, bits):
    for bit in reversed(bits):
        kept = value.shape[0] // 2
        got = swap(value[kept:].astype(jnp.bfloat16), axis, bit)
        value = value[:kept].astype(jnp.float32) + got.astype(jnp.float32)
    return value


def columns(value, bits):
    group = lax.axis_index("fsdp")
    for bit in bits:
        kept = value.shape[1] // 2
        low, high = value[:, :kept], value[:, kept:]
        upper = (group & bit) != 0
        mine, other = jnp.where(upper, high, low), jnp.where(upper, low, high)
        value = jnp.concatenate([mine, swap(other, "fsdp", bit)], axis=0)
    return value


def uncolumns(value, bits):
    group = lax.axis_index("fsdp")
    for bit in reversed(bits):
        kept = value.shape[0] // 2
        mine, other = value[:kept], swap(value[kept:], "fsdp", bit)
        upper = (group & bit) != 0
        value = jnp.concatenate(
            [jnp.where(upper, other, mine), jnp.where(upper, mine, other)], axis=1
        )
    return value


def layer(held, learner_rows, exponents, encode_more):
    experts, parts, unit_rows, width = learner_rows.shape
    groups = lax.axis_size("fsdp")
    x_bits, group_bits = low_bits("expert"), masks("fsdp")
    units = experts * unit_rows
    rows = held.shape[0]
    slots = rows << len(x_bits)

    table = held[:, groups * width :]
    held = columns(held[:, : groups * width], group_bits).reshape(groups, rows, width)
    pair = dequantize(learner_rows, exponents, 0, 2)

    def swap_all(values, bit):
        rows = [value.reshape(-1, width) for value in values]
        got = swap(jnp.concatenate(rows, axis=0), "expert", bit)
        ends = [sum(part.shape[0] for part in rows[:i]) for i in range(len(rows) + 1)]
        return [
            got[start:end].reshape(value.shape)
            for start, end, value in zip(ends, ends[1:], values)
        ]

    for bit in x_bits:
        got, got_table = swap_all([held, table], bit)
        held = jnp.concatenate([held, got], axis=1)
        table = jnp.concatenate([table, got_table], axis=0)
    held, pair, table = together(held, pair, table)
    partial = lax.dot_general(
        held.reshape(groups * slots, width),
        pair.reshape(-1, width),
        (((1,), (1,)), ((), ())),
        preferred_element_type=jnp.float32,
    ).astype(jnp.bfloat16)
    partial, table = together(partial, table)
    table = table[:, : 3 * experts].astype(jnp.float32).reshape(-1, 3, experts).sum(axis=1)

    down = dequantize(learner_rows, exponents, 2, 1)
    partial = halve(partial, "fsdp", group_bits)
    partial, down = together(partial, down)
    hidden = jax.nn.silu(partial[:, :units]) * partial[:, units:]
    shared = hidden.reshape(-1, experts, unit_rows) * table[:, :, None]
    shared = shared.astype(jnp.bfloat16).reshape(-1, units)
    shared, *more = together(gather(shared, "fsdp", group_bits), *encode_more())
    out = jnp.dot(shared, down.reshape(-1, width), preferred_element_type=jnp.float32)
    out = out.reshape(groups, slots, width)
    for bit in reversed(x_bits):
        kept = out.shape[1] // 2
        out = out[:, :kept] + swap(out[:, kept:].astype(jnp.bfloat16), "expert", bit)
    return out, *more


def body(tokens, learner_rows, exponents, expert_ids, route_probs):
    experts, parts, unit_rows, width = learner_rows.shape
    owners = lax.axis_size("expert")
    groups = lax.axis_size("fsdp")
    per_owner = experts // owners
    tok_rows = tokens.shape[0]
    bits, group_bits = masks("expert"), masks("fsdp")
    z_bits = bits[: len(bits) - len(low_bits("expert"))]
    me = lax.axis_index("expert").astype(jnp.int32).reshape(1)
    exponents = exponents.swapaxes(2, 3)

    half, low = bits[0], low_bits("expert")[0] * 2
    straight = list(range(half, owners, low))
    turning = [d for d in range(half, owners) if d % low]
    far = turning[: half // 4] + straight + turning[half // 4 :]
    first, second, third, fourth = (far[i * half // 4 : (i + 1) * half // 4] for i in range(4))
    begin = [d for d in range(low, half) if d % low]
    late = fourth + [d for d in range(1, half) if d not in begin]

    def blocks(partners, learner_rows, exponents):
        unit_rows = learner_rows.shape[2]
        return [
            encode(learner_rows, exponents, me, d, unit_rows, lambda m: 0) for d in partners
        ]

    early = first + second + third + begin
    sent, arrived = dict(zip(early, blocks(early, learner_rows, exponents))), {}

    def after(value, keys, table):
        value, *blocks = together(value, *[table[key] for key in keys])
        table.update(zip(keys, blocks))
        return value

    def send(keys):
        for key in keys:
            arrived[key] = swap(sent[key], "expert", key)

    table = after(share_table(expert_ids, route_probs, experts), first, sent)
    table = gather(table, "expert", z_bits[:1])
    held = gather(tokens, "expert", z_bits[:1])
    held = after(held, second, sent)
    held = jnp.concatenate([held, table], axis=1)
    held = gather(held, "expert", z_bits[1:])
    held = after(held, third + begin, sent)
    send(early)

    def serve(held, learner_rows, exponents):
        return layer(
            held, learner_rows, exponents, lambda: blocks(late, learner_rows, exponents)
        )

    def idle(held, learner_rows, exponents):
        out = jnp.zeros((groups, held.shape[0], width), jnp.float32)
        return out, *blocks(late, learner_rows, exponents)

    out, *got = lax.cond(expert_ids[0, 0] >= 0, serve, idle, held, learner_rows, exponents)
    sent.update(zip(late, got))
    out = after(out, first + second, arrived)

    out = out.reshape(groups, -1, tok_rows, width).swapaxes(0, 1)
    out = halve(out, "expert", z_bits[1:])
    out = after(out, begin, arrived)
    out = after(out, late, sent)
    send(late)
    out = halve(out, "expert", z_bits[:1])
    out = after(out, third, arrived)
    mixed = uncolumns(out.astype(jnp.bfloat16).reshape(groups * tok_rows, width), group_bits)

    elements = encode(learner_rows, exponents, me, 0, owners * unit_rows, lambda m: m)
    for partner in first + second + begin + third + late[len(fourth) :] + fourth:
        elements = place(elements, arrived[partner], me, partner)
    return elements.reshape(per_owner, parts, owners * unit_rows, width), mixed


def solution(mesh):
    return jax.shard_map(
        body,
        mesh=mesh,
        in_specs=(
            P(("fsdp", "expert"), None),
            P(None, None, "expert", "fsdp"),
            P(None, None, "expert", "fsdp"),
            P(("fsdp", "expert"), None),
            P(("fsdp", "expert"), None),
        ),
        out_specs=(P("expert", None, None, "fsdp"), P(("fsdp", "expert"), None)),
        check_vma=False,
    )
```
